256 devices in a mesh: island: 4 (over z_hi, core), fsdp: 64 (over x, y, z_lo).
Axes of the slice: x: 4, y: 4, z: 8 (z_hi: 2, z_lo: 4; z = z_hi * 4 + z_lo), core: 2. Of those that a mesh axis runs over, the one named last changes fastest.
Arguments:
- local_weights: float32 [4, 2, 2048, 7168], P('island', None, 'fsdp'), may hold values from -6.3 to 6.3, as said below
- first_moment: bfloat16 [4, 2, 2048, 7168], P('island', None, 'fsdp'), may hold values from -0.0014648438 to 0.0014648438
- second_moment: bfloat16 [4, 2, 2048, 7168], P('island', None, 'fsdp'), may hold values from 3.4015102e-10 to 1.359731e-07
- gradient: bfloat16 [4, 2, 2048, 7168], P('island', None, 'fsdp')
- anchor: float32 [2, 2048, 7168], P(None, 'fsdp'), may hold values from -6 to 6
- outer_momentum: float32 [2, 2048, 7168], P(None, 'fsdp'), may hold values from -0.4375 to 0.4375
- plan: int32 [2], replicated, may hold values from 0 to 1, as said below
- step_count: int32 [1], replicated, may hold values from 1 to 49
Outputs:
- weights_out: float32 [4, 2, 2048, 7168], P('island', None, 'fsdp')
- momentum_out: float32 [2, 2048, 7168], P(None, 'fsdp')
The draws below stay inside these ranges and needn't reach their ends.
Inputs may be any that keep to these rules, and one draw needn't show every extreme that they name: `plan`: exactly one entry is 1. `local_weights`: each replica's weights differ from the anchor by at most 0.3 in every entry.
All inputs are finite; a program needn't handle non-finite values.
Results may differ from the reference program's by a relative error of at most 0.007.
Values may be sent and summed in bfloat16 or wider, within the bound.
No kernel may reach another device: no remote copies, remote signals or barrier semaphores. Data moves between devices by JAX's collectives and lax.ppermute only.
A program may use at most 64 MiB of HBM per device.

```python
import math
import jax
import jax.numpy as jnp
from jax import lax

D = 2048
FF = 7168
FRAGS = 2
N_ISLAND = 4
N_FSDP = 64


def anchor_field(key):
    values = jax.random.normal(key, (FRAGS, D, FF), jnp.float32)
    return jnp.clip(values, -6.0, 6.0)


def draw_anchor(key, part):
    base = anchor_field(key)
    return base


def draw_local_weights(key, part):
    base = anchor_field(key)
    key = jax.random.fold_in(key, 5)
    keys = jax.random.split(key, 2)
    replica_scale = jnp.exp(jax.random.uniform(keys[0], (N_ISLAND, 1, 1, 1), jnp.float32, math.log(0.02), math.log(0.05)))
    drift = jnp.clip(jax.random.normal(keys[1], (N_ISLAND, FRAGS, D, FF), jnp.float32), -6.0, 6.0)
    return base[None] + replica_scale * drift


def draw_gradient(key, part):
    key = jax.random.fold_in(key, 11)
    keys = jax.random.split(key, 5)
    shape = (N_ISLAND, FRAGS, D, FF)
    position = jnp.arange(D, dtype=jnp.float32) / max(D - 1, 1)
    row_scale = jnp.exp(jax.random.uniform(keys[0], (N_ISLAND, FRAGS, D, 1), jnp.float32) * math.log(3.2))
    col_scale = jnp.exp(jax.random.uniform(keys[1], (N_ISLAND, FRAGS, 1, FF), jnp.float32) * math.log(3.2))
    block_rows = D // N_FSDP
    block_gain = jnp.exp(jax.random.uniform(keys[4], (N_ISLAND, FRAGS, N_FSDP, 1), jnp.float32, math.log(1.0 / 12.0), math.log(12.0)))
    block_gain = jnp.repeat(block_gain, block_rows, axis=2)
    ramp = jnp.sqrt(1.0 + 2.0 * position)
    values = jax.random.normal(keys[2], shape, jnp.float32)
    values = values * ramp[None, None, :, None] * row_scale * col_scale * block_gain
    return values.astype(jnp.bfloat16)


def draw_plan(key, part):
    key = jax.random.fold_in(key, 23)
    chosen = jax.random.randint(key, (), 0, FRAGS)
    return (jnp.arange(FRAGS, dtype=jnp.int32) == chosen).astype(jnp.int32)


def block_scale(key, extent, cuts, low, top_value):
    def one(axis_at, parts):
        draws = jax.random.uniform(jax.random.fold_in(jax.random.fold_in(key, 6), axis_at), (parts,), jnp.float32, low / len(cuts), top_value / len(cuts))
        return jnp.repeat(jnp.exp(draws), extent[axis_at] // parts).reshape((-1,) + (1,) * (len(extent) - axis_at - 1))

    factor_of = one(*cuts[0])
    for cut in cuts[1:]:
        factor_of = factor_of * one(*cut)
    return factor_of


def scatter_about(rng, shape, scale, reach, pieces=(), kind=jnp.bfloat16):
    level = block_scale(rng, shape, pieces, -0.22, 0.18) if pieces else 1.0
    values = jax.random.normal(rng, shape, jnp.float32) * scale * level
    return jnp.minimum(jnp.maximum(values, -reach), reach).astype(kind)


def setup_inputs(seed: int = 0) -> dict:
    streams_of = jax.random.split(jax.random.key(seed), 9)
    return {
        "local_weights": draw_local_weights(jax.random.fold_in(streams_of[8], 71), 0),
        "first_moment": scatter_about(streams_of[1], (N_ISLAND, FRAGS, D, FF), ((FRAGS * D * FF) ** -0.5 / 2), 0.0014648438, ((0, 4), (2, 64))),
        "second_moment": jnp.clip(jnp.exp(math.log(1.3597309589385986e-07) - 5.990823 * jax.random.uniform(streams_of[2], (N_ISLAND, FRAGS, D, FF), jnp.float32) ** block_scale(streams_of[2], (N_ISLAND, FRAGS, D, FF), ((0, 4), (2, 64)), -0.2, 0.2)), 3.4015101846307516e-10, 1.3597309589385986e-07).astype(jnp.bfloat16),
        "gradient": draw_gradient(jax.random.fold_in(streams_of[8], 71), 0),
        "anchor": draw_anchor(jax.random.fold_in(streams_of[8], 71), 0),
        "outer_momentum": scatter_about(streams_of[5], (FRAGS, D, FF), 0.03, 0.4375, ((1, 64),), jnp.float32),
        "plan": draw_plan(jax.random.fold_in(streams_of[8], 71), 0),
        "step_count": jax.random.randint(streams_of[7], (1,), 1, 50).astype(jnp.int32),
    }


CLIP_NORM = 1.0
NORM_EPSILON = 1e-06
BETA_ONE = 0.9
BETA_TWO = 0.95
INNER_RATE = 0.03
WEIGHT_DECAY = 0.1
ADAM_EPSILON = 1e-08
OUTER_RATE = 0.7
NESTEROV = 0.9

def adam_step(weights, first_old, second_old, gradient_f, clip_factor, step_value):
    scaled = gradient_f * clip_factor
    first_new = BETA_ONE * first_old + (1.0 - BETA_ONE) * scaled
    second_new = BETA_TWO * second_old + (1.0 - BETA_TWO) * scaled * scaled
    step_float = step_value.astype(jnp.float32)
    first_hat = first_new / (1.0 - jnp.power(BETA_ONE, step_float))
    second_hat = second_new / (1.0 - jnp.power(BETA_TWO, step_float))
    return weights - INNER_RATE * (first_hat / (jnp.sqrt(second_hat) + ADAM_EPSILON) + WEIGHT_DECAY * weights)

def reference(local_weights, first_moment, second_moment, gradient, anchor, outer_momentum, plan, step_count):
    gradient_f = gradient.astype(jnp.float32)
    square = lax.optimization_barrier(jnp.sum(gradient_f * gradient_f, axis=(1, 2, 3), keepdims=True))
    clip_factor = jnp.minimum(1.0, CLIP_NORM / jnp.sqrt(square + NORM_EPSILON))
    local = adam_step(local_weights, first_moment.astype(jnp.float32), second_moment.astype(jnp.float32), gradient_f, clip_factor, step_count[0])
    pseudo = lax.optimization_barrier((anchor[None] - local).astype(jnp.bfloat16)).astype(jnp.float32)
    averaged = lax.optimization_barrier(jnp.sum(pseudo, axis=0)) / N_ISLAND
    momentum_new = NESTEROV * outer_momentum + averaged
    anchor_new = anchor - OUTER_RATE * (averaged + NESTEROV * momentum_new)
    sync_flags = (plan > 0)[:, None, None]
    weights_out = jnp.where(sync_flags[None], anchor_new[None], local)
    momentum_out = jnp.where(sync_flags, momentum_new, outer_momentum)
    return (weights_out, momentum_out)
```

```python
import functools
import math

import jax
import jax.numpy as jnp
from jax import lax
from jax.experimental import pallas as pl
from jax.experimental.pallas import tpu as pltpu
from jax.sharding import PartitionSpec as P

CLIP_NORM = 1.0
NORM_EPSILON = 1e-06
BETA_ONE = 0.9
BETA_TWO = 0.95
INNER_RATE = 0.03
WEIGHT_DECAY = 0.1
ADAM_EPSILON = 1e-08
OUTER_RATE = 0.7
NESTEROV = 0.9

CHUNKS = 2
STEP = 512
VMEM_LIMIT = 40 * 1024 * 1024

ANY = pl.BlockSpec(memory_space=pl.ANY)
VMEM = pl.BlockSpec(memory_space=pltpu.VMEM)
SMEM = pl.BlockSpec(memory_space=pltpu.SMEM)
F32, BF16 = jnp.float32, jnp.bfloat16


def call(kernel, out_shape, in_specs, out_specs, scratch, cost, aliases=None):
    flops, size = cost
    return pl.pallas_call(
        kernel,
        out_shape=out_shape,
        in_specs=in_specs,
        out_specs=out_specs,
        scratch_shapes=scratch,
        input_output_aliases=aliases or {},
        compiler_params=pltpu.CompilerParams(vmem_limit_bytes=VMEM_LIMIT),
        cost_estimate=pl.CostEstimate(flops=flops, bytes_accessed=size, transcendentals=0),
    )


def spread(vector, width):
    return jnp.concatenate([jnp.broadcast_to(vector, (16, 128))] * (width // 128), axis=1)


def adam_factors(sums_ref, step_ref):
    square = jnp.sum(sums_ref[...], axis=0)
    clip = jnp.minimum(1.0, CLIP_NORM / jnp.sqrt(square + NORM_EPSILON))
    step = jnp.full((1, 128), step_ref[0].astype(F32))
    first = INNER_RATE / (1.0 - jnp.exp(step * math.log(BETA_ONE)))
    second = 1.0 / (1.0 - jnp.exp(step * math.log(BETA_TWO)))
    return (
        clip,
        BETA_ONE * first,
        (1.0 - BETA_ONE) * first,
        BETA_TWO * second,
        (1.0 - BETA_TWO) * second,
    )


def adam(weights, first, second, gradient, factors):
    clip, a, b, c, d = factors
    scaled = gradient.astype(F32) * clip
    numerator = a * first.astype(F32) + b * scaled
    square = c * second.astype(F32) + d * (scaled * scaled)
    return (1.0 - INNER_RATE * WEIGHT_DECAY) * weights - numerator / (
        jnp.sqrt(square) + ADAM_EPSILON
    )


def squares_kernel(gradient, out, buffer, sems):
    copies = []
    for i in range(2):
        copies.append(pltpu.make_async_copy(gradient.at[0, i], buffer.at[i], sems.at[i]))
        copies[-1].start()
    total = jnp.zeros((32, STEP), F32)
    for i in range(2):
        copies[i].wait()

        def body(k, total, i=i):
            block = buffer[i, :, pl.ds(pl.multiple_of(k * STEP, STEP), STEP)].astype(F32)
            return total + block * block

        total = lax.fori_loop(0, buffer.shape[2] // STEP, body, total)
    out[...] = jnp.full(out.shape, jnp.sum(total))


def pseudo_kernel(
    column, plan, step, sums, weights, first, second, gradient, anchor, keep, send, *scratch
):
    fragment = plan[1]
    core = lax.rem(lax.axis_index("island"), 2)
    buffers, sems = scratch[:-1], scratch[-1]
    width = keep.shape[1]
    sources = (
        weights.at[0, fragment],
        first.at[0, fragment],
        second.at[0, fragment],
        gradient.at[0, fragment],
        anchor.at[fragment],
    )
    copies = []
    for part, half in enumerate((1 - core, core)):
        row = pl.multiple_of(half * 16, 16)
        for i, source in enumerate(sources):
            copy = pltpu.make_async_copy(
                source.at[pl.ds(row, 16), pl.ds(column, width)], buffers[i].at[part], sems.at[part, i]
            )
            copy.start()
            copies.append(copy)
    factors = tuple(spread(f, STEP) for f in adam_factors(sums, step))
    for part, out in enumerate((send, keep)):
        for copy in copies[part * 5 : part * 5 + 5]:
            copy.wait()

        def body(k, _, part=part, out=out):
            at = pl.ds(pl.multiple_of(k * STEP, STEP), STEP)
            w, m, v, g, a = (buffer[part, :, at] for buffer in buffers)
            out[:, at] = (a - adam(w, m, v, g, factors)).astype(BF16)
            return 0

        lax.fori_loop(0, width // STEP, body, 0)


def add_kernel(one, two, out):
    out[...] = (one[...].astype(F32) + two[...].astype(F32)).astype(BF16)


def rest_kernel(
    plan, step, sums, weights, first, second, gradient, momentum, weights_out, momentum_out, *scratch
):
    fragment = 1 - plan[1]
    buffers, result, sems, out_sem = scratch[:-3], scratch[-3], scratch[-2], scratch[-1]
    kept = pltpu.make_async_copy(momentum.at[fragment], momentum_out.at[fragment], out_sem.at[2])
    kept.start()
    sources = (weights, first, second, gradient)
    copies = []
    for part in range(2):
        for i, source in enumerate(sources):
            copy = pltpu.make_async_copy(
                source.at[0, fragment, pl.ds(part * 16, 16)], buffers[i].at[part], sems.at[part, i]
            )
            copy.start()
            copies.append(copy)
    factors = tuple(spread(f, STEP) for f in adam_factors(sums, step))
    outs = []
    for part in range(2):
        for copy in copies[part * 4 : part * 4 + 4]:
            copy.wait()

        def body(k, _, part=part):
            at = pl.ds(pl.multiple_of(k * STEP, STEP), STEP)
            w, m, v, g = (buffer[part, :, at] for buffer in buffers)
            result[part, :, at] = adam(w, m, v, g, factors)
            return 0

        lax.fori_loop(0, result.shape[2] // STEP, body, 0)
        outs.append(
            pltpu.make_async_copy(
                result.at[part], weights_out.at[0, fragment, pl.ds(part * 16, 16)], out_sem.at[part]
            )
        )
        outs[-1].start()
    for copy in outs:
        copy.wait()
    kept.wait()


def outer_kernel(
    column, mine, plan, one, two, anchor, momentum, _, __, weights_out, momentum_out, *scratch
):
    anchors, momenta, sems, out_sems = scratch
    fragment = plan[1]
    core = lax.rem(lax.axis_index("island"), 2)
    row = pl.multiple_of((core if mine else 1 - core) * 16, 16)
    at = (fragment, pl.ds(row, 16), pl.ds(column, one.shape[1]))
    copies = [
        pltpu.make_async_copy(anchor.at[at], anchors, sems.at[0]),
        pltpu.make_async_copy(momentum.at[at], momenta, sems.at[1]),
    ]
    for copy in copies:
        copy.start()
    for copy in copies:
        copy.wait()

    def body(k, _):
        cols = pl.ds(pl.multiple_of(k * STEP, STEP), STEP)
        averaged = (one[:, cols].astype(F32) + two[:, cols].astype(F32)) * 0.25
        momentum_new = NESTEROV * momenta[:, cols] + averaged
        anchors[:, cols] = anchors[:, cols] - OUTER_RATE * (averaged + NESTEROV * momentum_new)
        momenta[:, cols] = momentum_new
        return 0

    lax.fori_loop(0, one.shape[1] // STEP, body, 0)
    outs = [
        pltpu.make_async_copy(anchors, weights_out.at[(0, *at)], out_sems.at[0]),
        pltpu.make_async_copy(momenta, momentum_out.at[at], out_sems.at[1]),
    ]
    for copy in outs:
        copy.start()
    for copy in outs:
        copy.wait()


def swap(x, bit):
    return lax.ppermute(x, "island", [(i, i ^ bit) for i in range(lax.axis_size("island"))])


def on_device(
    local_weights, first_moment, second_moment, gradient, anchor, outer_momentum, plan, step_count
):
    rows, columns = anchor.shape[1:]
    width = columns // CHUNKS
    owners = lax.axis_size("fsdp")
    shape = jax.ShapeDtypeStruct
    dma = pltpu.SemaphoreType.DMA
    buffer = pltpu.VMEM

    squares = call(
        squares_kernel,
        shape((owners, 1, 128), F32),
        [ANY],
        VMEM,
        [buffer((2, rows, columns), BF16), dma((2,))],
        (4 * rows * columns, 4 * rows * columns),
    )(gradient)
    sums = lax.all_to_all(squares, "fsdp", 0, 0)

    adam_args = (local_weights, first_moment, second_moment, gradient)
    parts = []
    for j in range(CHUNKS):
        keep, send = call(
            functools.partial(pseudo_kernel, j * width),
            [shape((16, width), BF16)] * 2,
            [SMEM, SMEM, VMEM] + [ANY] * 5,
            [VMEM, VMEM],
            [
                buffer((2, 16, width), F32),
                buffer((2, 16, width), BF16),
                buffer((2, 16, width), BF16),
                buffer((2, 16, width), BF16),
                buffer((2, 16, width), F32),
                dma((2, 5)),
            ],
            (25 * rows * width, 16 * rows * width),
        )(plan, step_count, sums, *adam_args, anchor)
        parts.append((keep, swap(send, 1)))

    mine, theirs = [], []
    for keep, got in parts:
        summed = call(
            add_kernel,
            shape((16, width), BF16),
            [VMEM, VMEM],
            VMEM,
            [],
            (16 * width, 96 * width),
        )(keep, got)
        far = swap(summed, 2)
        mine.append((summed, far))
        theirs.append((swap(summed, 1), swap(far, 1)))

    outs = call(
        rest_kernel,
        [shape(local_weights.shape, F32), shape(anchor.shape, F32)],
        [SMEM, SMEM, VMEM] + [ANY] * 5,
        [ANY, ANY],
        [
            buffer((2, 16, columns), F32),
            buffer((2, 16, columns), BF16),
            buffer((2, 16, columns), BF16),
            buffer((2, 16, columns), BF16),
            buffer((2, 16, columns), F32),
            dma((2, 4)),
            dma((3,)),
        ],
        (25 * rows * columns, 22 * rows * columns),
    )(plan, step_count, sums, *adam_args, outer_momentum)

    for j in range(CHUNKS):
        for own, (one, two) in ((True, mine[j]), (False, theirs[j])):
            outs = call(
                functools.partial(outer_kernel, j * width, own),
                [shape(local_weights.shape, F32), shape(anchor.shape, F32)],
                [SMEM, VMEM, VMEM] + [ANY] * 4,
                [ANY, ANY],
                [buffer((16, width), F32), buffer((16, width), F32), dma((2,)), dma((2,))],
                (8 * 16 * width, 20 * 16 * width),
                {5: 0, 6: 1},
            )(plan, one, two, anchor, outer_momentum, *outs)
    return tuple(outs)


def solution(mesh):
    return jax.shard_map(
        on_device,
        mesh=mesh,
        in_specs=(
            P("island", None, "fsdp", None),
            P("island", None, "fsdp", None),
            P("island", None, "fsdp", None),
            P("island", None, "fsdp", None),
            P(None, "fsdp", None),
            P(None, "fsdp", None),
            P(),
            P(),
        ),
        out_specs=(P("island", None, "fsdp", None), P(None, "fsdp", None)),
        check_vma=False,
    )
```

```python
import functools
import math

import jax
import jax.numpy as jnp
from jax import lax
from jax.experimental import pallas as pl
from jax.experimental.pallas import tpu as pltpu
from jax.sharding import PartitionSpec as P

CLIP_NORM = 1.0
NORM_EPSILON = 1e-06
BETA_ONE = 0.9
BETA_TWO = 0.95
INNER_RATE = 0.03
WEIGHT_DECAY = 0.1
ADAM_EPSILON = 1e-08
OUTER_RATE = 0.7
NESTEROV = 0.9

CHUNKS = 2
STEP = 512
VMEM_LIMIT = 16 * 1024 * 1024
HIDDEN = 40_000_000

HBM = pl.BlockSpec(memory_space=pltpu.HBM)
VMEM = pl.BlockSpec(memory_space=pltpu.VMEM)
SMEM = pl.BlockSpec(memory_space=pltpu.SMEM)
F32, BF16 = jnp.float32, jnp.bfloat16


def call(kernel, out_shape, in_specs, out_specs, scratch, cost, aliases=None):
    flops, size = cost
    return pl.pallas_call(
        kernel,
        out_shape=out_shape,
        in_specs=in_specs,
        out_specs=out_specs,
        scratch_shapes=scratch,
        input_output_aliases=aliases or {},
        compiler_params=pltpu.CompilerParams(vmem_limit_bytes=VMEM_LIMIT),
        cost_estimate=pl.CostEstimate(flops=flops, bytes_accessed=size, transcendentals=0),
    )


def spread(vector, width):
    return jnp.concatenate([jnp.broadcast_to(vector, (16, 128))] * (width // 128), axis=1)


def columns_of(k):
    return pl.ds(pl.multiple_of(k * STEP, STEP), STEP)


def moment_factors(step_ref):
    step = jnp.full((1, 128), step_ref[0].astype(F32))
    first = INNER_RATE / (1.0 - jnp.exp(step * math.log(BETA_ONE)))
    second = 1.0 / (1.0 - jnp.exp(step * math.log(BETA_TWO)))
    rows = (
        BETA_ONE * first,
        (1.0 - BETA_ONE) * first,
        BETA_TWO * second,
        (1.0 - BETA_TWO) * second,
    )
    return jnp.concatenate(rows * 2, axis=0)


def adam_factors(sums_ref, factors_ref):
    square = jnp.sum(jnp.sum(sums_ref[...], axis=0), axis=1, keepdims=True)
    clip = jnp.minimum(1.0, CLIP_NORM / jnp.sqrt(jnp.broadcast_to(square, (1, 128)) + NORM_EPSILON))
    return tuple(spread(row, STEP) for row in (clip, *(factors_ref[i : i + 1] for i in range(4))))


def adam_change(first, second, gradient, factors):
    clip, a, b, c, d = factors
    scaled = gradient.astype(F32) * clip
    numerator = a * first.astype(F32) + b * scaled
    square = c * second.astype(F32) + d * (scaled * scaled)
    return numerator / (square * lax.rsqrt(square) + ADAM_EPSILON)


def squares_kernel(gradient, kept, out, sems):
    copies = []
    for i in range(2):
        copies.append(pltpu.make_async_copy(gradient.at[0, i], kept.at[i], sems.at[i]))
        copies[-1].start()
    total = jnp.zeros((32, STEP), F32)
    for i in range(2):
        copies[i].wait()

        def body(k, total, i=i):
            block = kept[i, :, columns_of(k)].astype(F32)
            return total + block * block

        total = lax.fori_loop(0, kept.shape[2] // STEP, body, total)
    row = sum(total[:, i * 128 : i * 128 + 128] for i in range(STEP // 128))
    row = jnp.sum(row, axis=0, keepdims=True)
    out[...] = jnp.broadcast_to(row[None], out.shape)


def halves():
    core = lax.rem(lax.axis_index("island"), 2)
    return pl.multiple_of((1 - core) * 16, 16), pl.multiple_of(core * 16, 16)


def prepare_kernel(
    plan, step, weights, first, second, anchor, base, firsts, seconds, factors, weight, anchors, sems
):
    fragment = plan[1]
    copies = []
    for part, row in enumerate(halves()):
        rows = pl.ds(row, 16)
        pairs = (
            (weights.at[0, fragment, rows], weight.at[part]),
            (anchor.at[fragment, rows], anchors.at[part]),
            (first.at[0, fragment, rows], firsts.at[part]),
            (second.at[0, fragment, rows], seconds.at[part]),
        )
        for i, (source, target) in enumerate(pairs):
            copies.append(pltpu.make_async_copy(source, target, sems.at[part, i]))
            copies[-1].start()
    factors[...] = moment_factors(step)
    for part in range(2):
        for copy in copies[part * 4 : part * 4 + 4]:
            copy.wait()

        def body(k, _, part=part):
            at = columns_of(k)
            decayed = (1.0 - INNER_RATE * WEIGHT_DECAY) * weight[part, :, at]
            base[part, :, at] = anchors[part, :, at] - decayed
            return 0

        lax.fori_loop(0, base.shape[2] // STEP, body, 0, unroll=True)


def pseudo_kernel(part, plan, factors, sums, base, first, second, gradient, out):
    fragment, rows = plan[1], pl.ds(halves()[part], 16)
    factors = adam_factors(sums, factors)

    def body(k, _):
        at = columns_of(k)
        change = adam_change(first[part, :, at], second[part, :, at], gradient[fragment, rows, at], factors)
        out[:, at] = (base[part, :, at] + change).astype(BF16)
        return 0

    lax.fori_loop(0, out.shape[1] // STEP, body, 0, unroll=True)


def add_kernel(one, two, out):
    out[...] = (one[...].astype(F32) + two[...].astype(F32)).astype(BF16)


def rest_kernel(
    plan, factors, sums, gradient, _, weights, first, second, anchor, momentum, weights_out, momentum_out, base, momenta, *scratch
):
    fragment = 1 - plan[1]
    buffers, (result, anchors, still, sems, out_sem) = scratch[:3], scratch[3:]
    sources = (weights, first, second)
    copies = []
    for part in range(2):
        for i, source in enumerate(sources):
            copies.append(
                pltpu.make_async_copy(
                    source.at[0, fragment, pl.ds(part * 16, 16)], buffers[i].at[part], sems.at[part, i]
                )
            )
    for part, row in enumerate(halves()):
        rows = pl.ds(row, 16)
        copies.append(pltpu.make_async_copy(anchor.at[1 - fragment, rows], anchors.at[part], sems.at[part, 3]))
        copies.append(pltpu.make_async_copy(momentum.at[1 - fragment, rows], momenta.at[part], sems.at[part, 4]))
    for copy in copies:
        copy.start()
    kept = pltpu.make_async_copy(momentum.at[fragment], still, out_sem.at[2])
    kept.start()
    factors = adam_factors(sums, factors)
    outs = []
    for part in range(2):
        for copy in copies[part * 3 : part * 3 + 3]:
            copy.wait()

        def body(k, _, part=part):
            at = columns_of(k)
            w, m, v = (buffer[part, :, at] for buffer in buffers)
            change = adam_change(m, v, gradient[fragment, pl.ds(part * 16, 16), at], factors)
            result[part, :, at] = (1.0 - INNER_RATE * WEIGHT_DECAY) * w - change
            return 0

        lax.fori_loop(0, result.shape[2] // STEP, body, 0, unroll=True)
        outs.append(
            pltpu.make_async_copy(
                result.at[part], weights_out.at[0, fragment, pl.ds(part * 16, 16)], out_sem.at[part]
            )
        )
        outs[-1].start()
    kept.wait()
    outs.append(pltpu.make_async_copy(still, momentum_out.at[fragment], out_sem.at[3]))
    outs[-1].start()
    for part in range(2):
        for copy in copies[6 + 2 * part : 8 + 2 * part]:
            copy.wait()

        def outer(k, _, part=part):
            at = columns_of(k)
            m = momenta[part, :, at]
            base[part, :, at] = anchors[part, :, at] - (OUTER_RATE * NESTEROV * NESTEROV) * m
            momenta[part, :, at] = NESTEROV * m
            return 0

        lax.fori_loop(0, result.shape[2] // STEP, outer, 0, unroll=True)
    for copy in outs:
        copy.wait()


def outer_kernel(part, plan, one, two, base, momenta, _, __, weights_out, momentum_out, weight, moment, sems):
    width = one.shape[1] // CHUNKS
    rows = pl.ds(halves()[part], 16)
    outs = []
    for j in range(CHUNKS):

        def body(k, _, j=j):
            at = pl.ds(pl.multiple_of(j * width + k * STEP, STEP), STEP)
            averaged = (one[:, at].astype(F32) + two[:, at].astype(F32)) * 0.25
            weight[:, at] = base[part, :, at] - (OUTER_RATE * (1.0 + NESTEROV)) * averaged
            moment[:, at] = momenta[part, :, at] + averaged
            return 0

        lax.fori_loop(0, width // STEP, body, 0, unroll=True)
        at = pl.ds(j * width, width)
        outs += [
            pltpu.make_async_copy(weight.at[:, at], weights_out.at[0, plan[1], rows, at], sems.at[j, 0]),
            pltpu.make_async_copy(moment.at[:, at], momentum_out.at[plan[1], rows, at], sems.at[j, 1]),
        ]
        for copy in outs[-2:]:
            copy.start()
    for copy in outs:
        copy.wait()


def swap(x, bit):
    return lax.ppermute(x, "island", [(i, i ^ bit) for i in range(lax.axis_size("island"))])


def on_device(
    local_weights, first_moment, second_moment, gradient, anchor, outer_momentum, plan, step_count
):
    local_weights, first_moment, second_moment, gradient, anchor, outer_momentum = (
        pltpu.with_memory_space_constraint(x, pltpu.HBM)
        for x in (local_weights, first_moment, second_moment, gradient, anchor, outer_momentum)
    )
    rows, columns = anchor.shape[1:]
    owners = lax.axis_size("fsdp")
    shape = jax.ShapeDtypeStruct
    dma = pltpu.SemaphoreType.DMA
    buffer = pltpu.VMEM
    two = (2, 16, columns)

    kept, squares = call(
        squares_kernel,
        [shape((2, rows, columns), BF16), shape((owners, 1, 128), F32)],
        [HBM],
        [VMEM, VMEM],
        [dma((2,))],
        (4 * rows * columns, 4 * rows * columns),
    )(gradient)
    sums = lax.all_to_all(squares, "fsdp", 0, 0)
    base, firsts, seconds, factors = call(
        prepare_kernel,
        [shape(two, F32), shape(two, BF16), shape(two, BF16), shape((8, 128), F32)],
        [SMEM, SMEM] + [HBM] * 4,
        [VMEM] * 4,
        [buffer(two, F32), buffer(two, F32), dma((2, 4))],
        (HIDDEN, HIDDEN),
    )(plan, step_count, local_weights, first_moment, second_moment, anchor)

    send, keep = (
        call(
            functools.partial(pseudo_kernel, part),
            shape((16, columns), BF16),
            [SMEM] + [VMEM] * 6,
            VMEM,
            [],
            (HIDDEN, HIDDEN) if part else (12 * rows * columns, 5 * rows * columns),
        )(plan, factors, sums, base, firsts, seconds, kept)
        for part in (0, 1)
    )
    summed = call(
        add_kernel,
        shape((16, columns), BF16),
        [VMEM, VMEM],
        VMEM,
        [],
        (16 * columns, 96 * columns),
    )(keep, swap(send, 1))
    far, theirs = swap(summed, 2), swap(summed, 1)

    *outs, outer_base, outer_momenta = call(
        rest_kernel,
        [shape(local_weights.shape, F32), shape(anchor.shape, F32), shape(two, F32), shape(two, F32)],
        [SMEM] + [VMEM] * 4 + [HBM] * 5,
        [HBM, HBM, VMEM, VMEM],
        [
            buffer(two, F32),
            buffer(two, BF16),
            buffer(two, BF16),
            buffer(two, F32),
            buffer(two, F32),
            buffer((rows, columns), F32),
            dma((2, 5)),
            dma((4,)),
        ],
        (HIDDEN, HIDDEN),
    )(plan, factors, sums, kept, summed, local_weights, first_moment, second_moment, anchor, outer_momentum)

    far, outer_base = lax.optimization_barrier((far, outer_base))
    for part, one, other in ((1, summed, far), (0, theirs, swap(far, 1))):
        outs = call(
            functools.partial(outer_kernel, part),
            [shape(local_weights.shape, F32), shape(anchor.shape, F32)],
            [SMEM] + [VMEM] * 4 + [HBM] * 2,
            [HBM, HBM],
            [buffer((16, columns), F32), buffer((16, columns), F32), dma((CHUNKS, 2))],
            (HIDDEN, HIDDEN) if part else (1, 1),
            {5: 0, 6: 1},
        )(plan, one, other, outer_base, outer_momenta, *outs)
    return tuple(outs)


def solution(mesh):
    return jax.shard_map(
        on_device,
        mesh=mesh,
        in_specs=(
            P("island", None, "fsdp", None),
            P("island", None, "fsdp", None),
            P("island", None, "fsdp", None),
            P("island", None, "fsdp", None),
            P(None, "fsdp", None),
            P(None, "fsdp", None),
            P(),
            P(),
        ),
        out_specs=(P("island", None, "fsdp", None), P(None, "fsdp", None)),
        check_vma=False,
    )
```

```python
import functools
import math
import random

import jax
import jax.numpy as jnp
from jax import lax
from jax.experimental import pallas as pl
from jax.experimental.pallas import tpu as pltpu
from jax.sharding import PartitionSpec as P

CLIP_NORM = 1.0
NORM_EPSILON = 1e-06
BETA_ONE = 0.9
BETA_TWO = 0.95
INNER_RATE = 0.03
WEIGHT_DECAY = 0.1
ADAM_EPSILON = 1e-08
OUTER_RATE = 0.7
NESTEROV = 0.9

PIECES = 4
CHUNKS = 2
STEP = 512
VMEM_LIMIT = 16 * 1024 * 1024
HIDDEN = 40_000_000

HBM = pl.BlockSpec(memory_space=pltpu.HBM)
VMEM = pl.BlockSpec(memory_space=pltpu.VMEM)
SMEM = pl.BlockSpec(memory_space=pltpu.SMEM)
F32, BF16 = jnp.float32, jnp.bfloat16


def call(kernel, out_shape, in_specs, out_specs, scratch, cost, aliases=None):
    flops, size = cost
    return pl.pallas_call(
        kernel,
        out_shape=out_shape,
        in_specs=in_specs,
        out_specs=out_specs,
        scratch_shapes=scratch,
        input_output_aliases=aliases or {},
        compiler_params=pltpu.CompilerParams(vmem_limit_bytes=VMEM_LIMIT),
        cost_estimate=pl.CostEstimate(flops=flops, bytes_accessed=size, transcendentals=0),
    )


def spread(vector, width):
    return jnp.concatenate([jnp.broadcast_to(vector, (16, 128))] * (width // 128), axis=1)


def columns_of(k):
    return pl.ds(pl.multiple_of(k * STEP, STEP), STEP)


def factors_kernel(step, factors):
    step = jnp.full((1, 128), step[0].astype(F32))
    first = INNER_RATE / (1.0 - jnp.exp(step * math.log(BETA_ONE)))
    second = 1.0 / (1.0 - jnp.exp(step * math.log(BETA_TWO)))
    rows = (
        BETA_ONE * first,
        (1.0 - BETA_ONE) * first,
        BETA_TWO * second,
        (1.0 - BETA_TWO) * second,
    )
    factors[...] = jnp.concatenate(rows * 2, axis=0)


def adam_factors(sums_ref, factors_ref):
    square = jnp.sum(jnp.sum(sums_ref[...], axis=0, keepdims=True), axis=1, keepdims=True)
    clip = jnp.minimum(1.0, CLIP_NORM / jnp.sqrt(jnp.broadcast_to(square, (1, 128)) + NORM_EPSILON))
    return tuple(spread(row, STEP) for row in (clip, *(factors_ref[i : i + 1] for i in range(4))))


def adam_change(first, second, gradient, factors):
    clip, a, b, c, d = factors
    scaled = gradient.astype(F32) * clip
    numerator = a * first.astype(F32) + b * scaled
    square = c * second.astype(F32) + d * (scaled * scaled)
    return numerator / (square * lax.rsqrt(square) + ADAM_EPSILON)


def halves():
    core = lax.rem(lax.axis_index("island"), 2)
    return pl.multiple_of((1 - core) * 16, 16), pl.multiple_of(core * 16, 16)


def squares_kernel(plan, gradient, squares, chosen, whole, sems, plan_sem):
    plan_copy = pltpu.make_async_copy(plan, chosen, plan_sem.at[0])
    plan_copy.start()
    width = whole.shape[2] // PIECES
    pieces = [(i, pl.ds(j * width, width)) for i in range(2) for j in range(PIECES)]
    copies = []
    for n, (i, at) in enumerate(pieces):
        copies.append(pltpu.make_async_copy(gradient.at[0, i, :, at], whole.at[i, :, at], sems.at[n]))
        copies[-1].start()
    total = jnp.zeros((32, 256), F32)
    for copy, (i, at) in zip(copies, pieces, strict=True):
        copy.wait()
        for k in range(width // 256):
            block = whole[i, :, pl.ds(at.start + k * 256, 256)].astype(F32)
            total = total + block * block
    row = jnp.sum(total[:, :128] + total[:, 128:], axis=0, keepdims=True)
    squares[...] = jnp.broadcast_to(row, squares.shape)
    plan_copy.wait()


def prepare_kernel(
    plan, weights, first, second, gradient, anchor, base, firsts, seconds, gradients, weight, anchors, sems
):
    fragment = plan[1]
    copies = []
    for part, row in enumerate(halves()):
        rows = pl.ds(row, 16)
        pairs = (
            (weights.at[0, fragment, rows], weight.at[part]),
            (anchor.at[fragment, rows], anchors.at[part]),
            (first.at[0, fragment, rows], firsts.at[part]),
            (second.at[0, fragment, rows], seconds.at[part]),
            (gradient.at[0, fragment, rows], gradients.at[part]),
        )
        for i, (source, target) in enumerate(pairs):
            copies.append(pltpu.make_async_copy(source, target, sems.at[part, i]))
            copies[-1].start()
    for part in range(2):
        for copy in copies[part * 5 : part * 5 + 5]:
            copy.wait()

        def body(k, _, part=part):
            at = columns_of(k)
            decayed = (1.0 - INNER_RATE * WEIGHT_DECAY) * weight[part, :, at]
            base[part, :, at] = anchors[part, :, at] - decayed
            return 0

        lax.fori_loop(0, base.shape[2] // STEP, body, 0, unroll=True)


def pseudo_kernel(part, factors, sums, base, first, second, gradient, out):
    factors = adam_factors(sums, factors)

    def body(k, _):
        at = columns_of(k)
        change = adam_change(first[part, :, at], second[part, :, at], gradient[part, :, at], factors)
        out[:, at] = (base[part, :, at] + change).astype(BF16)
        return 0

    lax.fori_loop(0, out.shape[1] // STEP, body, 0, unroll=True)


def add_kernel(one, two, out):
    out[...] = (one[...].astype(F32) + two[...].astype(F32)).astype(BF16)


def rest_kernel(
    plan, factors, sums, _, gradient, weights, first, second, anchor, momentum, weights_out, momentum_out, base, momenta, *scratch
):
    fragment = 1 - plan[1]
    buffers, (result, anchors, still, sems, out_sem) = scratch[:4], scratch[4:]
    sources = (weights, first, second, gradient)
    copies = []
    for part in range(2):
        for i, source in enumerate(sources):
            copies.append(
                pltpu.make_async_copy(
                    source.at[0, fragment, pl.ds(part * 16, 16)], buffers[i].at[part], sems.at[part, i]
                )
            )
    for part, row in enumerate(halves()):
        rows = pl.ds(row, 16)
        copies.append(pltpu.make_async_copy(anchor.at[1 - fragment, rows], anchors.at[part], sems.at[part, 4]))
        copies.append(pltpu.make_async_copy(momentum.at[1 - fragment, rows], momenta.at[part], sems.at[part, 5]))
    for copy in copies:
        copy.start()
    kept = pltpu.make_async_copy(momentum.at[fragment], still, out_sem.at[2])
    kept.start()
    factors = adam_factors(sums, factors)
    outs = []
    for part in range(2):
        for copy in copies[part * 4 : part * 4 + 4]:
            copy.wait()

        def body(k, _, part=part):
            at = columns_of(k)
            w, m, v, g = (buffer[part, :, at] for buffer in buffers)
            change = adam_change(m, v, g, factors)
            result[part, :, at] = (1.0 - INNER_RATE * WEIGHT_DECAY) * w - change
            return 0

        lax.fori_loop(0, result.shape[2] // STEP, body, 0, unroll=True)
        outs.append(
            pltpu.make_async_copy(
                result.at[part], weights_out.at[0, fragment, pl.ds(part * 16, 16)], out_sem.at[part]
            )
        )
        outs[-1].start()
    kept.wait()
    outs.append(pltpu.make_async_copy(still, momentum_out.at[fragment], out_sem.at[3]))
    outs[-1].start()
    for part in range(2):
        for copy in copies[8 + 2 * part : 10 + 2 * part]:
            copy.wait()

        def outer(k, _, part=part):
            at = columns_of(k)
            m = momenta[part, :, at]
            base[part, :, at] = anchors[part, :, at] - (OUTER_RATE * NESTEROV * NESTEROV) * m
            momenta[part, :, at] = NESTEROV * m
            return 0

        lax.fori_loop(0, result.shape[2] // STEP, outer, 0, unroll=True)
    for copy in outs:
        copy.wait()


def outer_kernel(part, plan, one, two, base, momenta, _, __, weights_out, momentum_out, weight, moment, sems):
    width = one.shape[1] // CHUNKS
    rows = pl.ds(halves()[part], 16)
    outs = []
    for j in range(CHUNKS):

        def body(k, _, j=j):
            at = pl.ds(pl.multiple_of(j * width + k * STEP, STEP), STEP)
            averaged = (one[:, at].astype(F32) + two[:, at].astype(F32)) * 0.25
            weight[:, at] = base[part, :, at] - (OUTER_RATE * (1.0 + NESTEROV)) * averaged
            moment[:, at] = momenta[part, :, at] + averaged
            return 0

        lax.fori_loop(0, width // STEP, body, 0, unroll=True)
        at = pl.ds(j * width, width)
        outs += [
            pltpu.make_async_copy(weight.at[:, at], weights_out.at[0, plan[1], rows, at], sems.at[j, 0]),
            pltpu.make_async_copy(moment.at[:, at], momentum_out.at[plan[1], rows, at], sems.at[j, 1]),
        ]
        for copy in outs[-2:]:
            copy.start()
    for copy in outs:
        copy.wait()


def owner_groups():
    def place(owner):
        x, y, z = owner // 16, owner // 4 % 4, owner % 4
        return z, min(x, 4 - x) + min(y, 4 - y)

    owners = list(range(64))
    random.Random(1).shuffle(owners)
    owners.sort(key=place, reverse=True)
    return [[island * 64 + owner for owner in owners] for island in range(4)]


def swap(x, bit):
    return lax.ppermute(x, "island", [(i, i ^ bit) for i in range(lax.axis_size("island"))])


def in_hbm(x):
    return pltpu.with_memory_space_constraint(x, pltpu.HBM)


def on_device(
    local_weights, first_moment, second_moment, gradient, anchor, outer_momentum, plan, step_count
):
    local_weights, first_moment, second_moment, gradient, anchor, outer_momentum = (
        in_hbm(x) for x in (local_weights, first_moment, second_moment, gradient, anchor, outer_momentum)
    )
    rows, columns = anchor.shape[1:]
    owners = lax.axis_size("fsdp")
    shape = jax.ShapeDtypeStruct
    dma = pltpu.SemaphoreType.DMA
    buffer = pltpu.VMEM
    two = (2, 16, columns)

    squares, chosen = call(
        squares_kernel,
        [shape((owners, 128), F32), pltpu.SMEM((2,), jnp.int32)],
        [HBM] * 2,
        [VMEM, SMEM],
        [buffer((2, rows, columns), BF16), dma((2 * PIECES,)), dma((1,))],
        (4 * rows * columns, 4 * rows * columns),
    )(in_hbm(plan), gradient)
    step_count, squares = lax.optimization_barrier((step_count, squares))
    sums = lax.all_to_all(
        squares.reshape(owners, 1, 128), ("island", "fsdp"), 0, 0, axis_index_groups=owner_groups()
    ).reshape(owners, 128)
    base, firsts, seconds, gradients = call(
        prepare_kernel,
        [shape(two, F32)] + [shape(two, BF16)] * 3,
        [SMEM] + [HBM] * 5,
        [VMEM] * 4,
        [buffer(two, F32), buffer(two, F32), dma((2, 5))],
        (HIDDEN, HIDDEN),
    )(chosen, local_weights, first_moment, second_moment, gradient, anchor)
    factors = call(factors_kernel, shape((8, 128), F32), [SMEM], VMEM, [], (HIDDEN, HIDDEN))(step_count)
    send, keep = (
        call(
            functools.partial(pseudo_kernel, part),
            shape((16, columns), BF16),
            [VMEM] * 6,
            VMEM,
            [],
            (HIDDEN, HIDDEN) if part else (12 * rows * columns, 5 * rows * columns),
        )(factors, sums, base, firsts, seconds, gradients)
        for part in (0, 1)
    )
    summed = call(
        add_kernel,
        shape((16, columns), BF16),
        [VMEM, VMEM],
        VMEM,
        [],
        (16 * columns, 96 * columns),
    )(keep, swap(send, 1))
    far, theirs = swap(summed, 2), swap(summed, 1)

    *outs, outer_base, outer_momenta = call(
        rest_kernel,
        [shape(local_weights.shape, F32), shape(anchor.shape, F32), shape(two, F32), shape(two, F32)],
        [SMEM] + [VMEM] * 3 + [HBM] * 6,
        [HBM, HBM, VMEM, VMEM],
        [
            buffer(two, F32),
            buffer(two, BF16),
            buffer(two, BF16),
            buffer(two, BF16),
            buffer(two, F32),
            buffer(two, F32),
            buffer((rows, columns), F32),
            dma((2, 6)),
            dma((4,)),
        ],
        (HIDDEN, HIDDEN),
    )(chosen, factors, sums, summed, gradient, local_weights, first_moment, second_moment, anchor, outer_momentum)

    far, outer_base = lax.optimization_barrier((far, outer_base))
    for part, one, other in ((1, summed, far), (0, theirs, swap(far, 1))):
        outs = call(
            functools.partial(outer_kernel, part),
            [shape(local_weights.shape, F32), shape(anchor.shape, F32)],
            [SMEM] + [VMEM] * 4 + [HBM] * 2,
            [HBM, HBM],
            [buffer((16, columns), F32), buffer((16, columns), F32), dma((CHUNKS, 2))],
            (HIDDEN, HIDDEN) if part else (1, 1),
            {5: 0, 6: 1},
        )(chosen, one, other, outer_base, outer_momenta, *outs)
    return tuple(outs)


def solution(mesh):
    return jax.shard_map(
        on_device,
        mesh=mesh,
        in_specs=(
            P("island", None, "fsdp", None),
            P("island", None, "fsdp", None),
            P("island", None, "fsdp", None),
            P("island", None, "fsdp", None),
            P(None, "fsdp", None),
            P(None, "fsdp", None),
            P(),
            P(),
        ),
        out_specs=(P("island", None, "fsdp", None), P(None, "fsdp", None)),
        check_vma=False,
    )
```

```python
import functools
import math
import random

import jax
import jax.numpy as jnp
from jax import lax
from jax.experimental import pallas as pl
from jax.experimental.pallas import tpu as pltpu
from jax.sharding import PartitionSpec as P

CLIP_NORM = 1.0
NORM_EPSILON = 1e-06
BETA_ONE = 0.9
BETA_TWO = 0.95
INNER_RATE = 0.03
WEIGHT_DECAY = 0.1
ADAM_EPSILON = 1e-08
OUTER_RATE = 0.7
NESTEROV = 0.9

PIECES = 4
CHUNKS = 2
STEP = 512
VMEM_LIMIT = 16 * 1024 * 1024
HIDDEN = 40_000_000

HBM = pl.BlockSpec(memory_space=pltpu.HBM)
VMEM = pl.BlockSpec(memory_space=pltpu.VMEM)
SMEM = pl.BlockSpec(memory_space=pltpu.SMEM)
F32, BF16 = jnp.float32, jnp.bfloat16


def call(kernel, out_shape, in_specs, out_specs, scratch, cost, aliases=None):
    flops, size = cost
    return pl.pallas_call(
        kernel,
        out_shape=out_shape,
        in_specs=in_specs,
        out_specs=out_specs,
        scratch_shapes=scratch,
        input_output_aliases=aliases or {},
        compiler_params=pltpu.CompilerParams(vmem_limit_bytes=VMEM_LIMIT),
        cost_estimate=pl.CostEstimate(flops=flops, bytes_accessed=size, transcendentals=0),
    )


def spread(vector, width):
    return jnp.concatenate([jnp.broadcast_to(vector, (16, 128))] * (width // 128), axis=1)


def columns_of(k):
    return pl.ds(pl.multiple_of(k * STEP, STEP), STEP)


def factors_kernel(step, factors):
    step = jnp.full((1, 128), step[0].astype(F32))
    first = INNER_RATE / (1.0 - jnp.exp(step * math.log(BETA_ONE)))
    second = 1.0 / (1.0 - jnp.exp(step * math.log(BETA_TWO)))
    rows = (
        BETA_ONE * first,
        (1.0 - BETA_ONE) * first,
        BETA_TWO * second,
        (1.0 - BETA_TWO) * second,
    )
    factors[...] = jnp.concatenate(rows * 2, axis=0)


def adam_factors(sums_ref, factors_ref):
    square = jnp.sum(jnp.sum(sums_ref[...], axis=0, keepdims=True), axis=1, keepdims=True)
    clip = jnp.minimum(1.0, CLIP_NORM / jnp.sqrt(jnp.broadcast_to(square, (1, 128)) + NORM_EPSILON))
    return tuple(spread(row, STEP) for row in (clip, *(factors_ref[i : i + 1] for i in range(4))))


def adam_change(first, second, gradient, factors):
    clip, a, b, c, d = factors
    scaled = gradient.astype(F32) * clip
    numerator = a * first.astype(F32) + b * scaled
    square = c * second.astype(F32) + d * (scaled * scaled)
    return numerator / (square * lax.rsqrt(square) + ADAM_EPSILON)


def halves():
    core = lax.rem(lax.axis_index("island"), 2)
    return pl.multiple_of((1 - core) * 16, 16), pl.multiple_of(core * 16, 16)


def squares_kernel(plan, gradient, squares, chosen, whole, sems, plan_sem):
    plan_copy = pltpu.make_async_copy(plan, chosen, plan_sem.at[0])
    plan_copy.start()
    width = whole.shape[2] // PIECES
    pieces = [(i, pl.ds(j * width, width)) for i in range(2) for j in range(PIECES)]
    copies = []
    for n, (i, at) in enumerate(pieces):
        copies.append(pltpu.make_async_copy(gradient.at[0, i, :, at], whole.at[i, :, at], sems.at[n]))
        copies[-1].start()
    total = jnp.zeros((32, 256), F32)
    for copy, (i, at) in zip(copies, pieces, strict=True):
        copy.wait()
        for k in range(width // 256):
            block = whole[i, :, pl.ds(at.start + k * 256, 256)].astype(F32)
            total = total + block * block
    row = jnp.sum(total[:, :128] + total[:, 128:], axis=0, keepdims=True)
    squares[...] = jnp.broadcast_to(row, squares.shape)
    plan_copy.wait()


def prepare_kernel(
    plan, weights, first, second, gradient, anchor, base, firsts, seconds, gradients, weight, anchors, sems
):
    fragment = plan[1]
    copies = []
    for part, row in enumerate(halves()):
        rows = pl.ds(row, 16)
        pairs = (
            (weights.at[0, fragment, rows], weight.at[part]),
            (anchor.at[fragment, rows], anchors.at[part]),
            (first.at[0, fragment, rows], firsts.at[part]),
            (second.at[0, fragment, rows], seconds.at[part]),
            (gradient.at[0, fragment, rows], gradients.at[part]),
        )
        for i, (source, target) in enumerate(pairs):
            copies.append(pltpu.make_async_copy(source, target, sems.at[part, i]))
            copies[-1].start()
    for part in range(2):
        for copy in copies[part * 5 : part * 5 + 5]:
            copy.wait()

        def body(k, _, part=part):
            at = columns_of(k)
            decayed = (1.0 - INNER_RATE * WEIGHT_DECAY) * weight[part, :, at]
            base[part, :, at] = anchors[part, :, at] - decayed
            return 0

        lax.fori_loop(0, base.shape[2] // STEP, body, 0, unroll=True)


def pseudo_kernel(part, factors, sums, base, first, second, gradient, out):
    factors = adam_factors(sums, factors)

    def body(k, _):
        at = columns_of(k)
        change = adam_change(first[part, :, at], second[part, :, at], gradient[part, :, at], factors)
        out[:, at] = (base[part, :, at] + change).astype(BF16)
        return 0

    lax.fori_loop(0, out.shape[1] // STEP, body, 0, unroll=True)


def add_kernel(one, two, out):
    out[...] = (one[...].astype(F32) + two[...].astype(F32)).astype(BF16)


def rest_kernel(
    plan, factors, sums, _, gradient, weights, first, second, anchor, momentum, weights_out, momentum_out, base, momenta, *scratch
):
    fragment = 1 - plan[1]
    buffers, (result, anchors, still, sems, out_sem) = scratch[:4], scratch[4:]
    sources = (weights, first, second, gradient)
    copies = []
    for part in range(2):
        for i, source in enumerate(sources):
            copies.append(
                pltpu.make_async_copy(
                    source.at[0, fragment, pl.ds(part * 16, 16)], buffers[i].at[part], sems.at[part, i]
                )
            )
    for part, row in enumerate(halves()):
        rows = pl.ds(row, 16)
        copies.append(pltpu.make_async_copy(anchor.at[1 - fragment, rows], anchors.at[part], sems.at[part, 4]))
        copies.append(pltpu.make_async_copy(momentum.at[1 - fragment, rows], momenta.at[part], sems.at[part, 5]))
    for copy in copies:
        copy.start()
    kept = pltpu.make_async_copy(momentum.at[fragment], still, out_sem.at[2])
    kept.start()
    factors = adam_factors(sums, factors)
    outs = []
    for part in range(2):
        for copy in copies[part * 4 : part * 4 + 4]:
            copy.wait()

        def body(k, _, part=part):
            at = columns_of(k)
            w, m, v, g = (buffer[part, :, at] for buffer in buffers)
            change = adam_change(m, v, g, factors)
            result[part, :, at] = (1.0 - INNER_RATE * WEIGHT_DECAY) * w - change
            return 0

        lax.fori_loop(0, result.shape[2] // STEP, body, 0, unroll=True)
        outs.append(
            pltpu.make_async_copy(
                result.at[part], weights_out.at[0, fragment, pl.ds(part * 16, 16)], out_sem.at[part]
            )
        )
        outs[-1].start()
    kept.wait()
    outs.append(pltpu.make_async_copy(still, momentum_out.at[fragment], out_sem.at[3]))
    outs[-1].start()
    for part in range(2):
        for copy in copies[8 + 2 * part : 10 + 2 * part]:
            copy.wait()

        def outer(k, _, part=part):
            at = columns_of(k)
            m = momenta[part, :, at]
            base[part, :, at] = anchors[part, :, at] - (OUTER_RATE * NESTEROV * NESTEROV) * m
            momenta[part, :, at] = NESTEROV * m
            return 0

        lax.fori_loop(0, result.shape[2] // STEP, outer, 0, unroll=True)
    for copy in outs:
        copy.wait()


def outer_kernel(part, plan, one, two, base, momenta, _, __, weights_out, momentum_out, weight, moment, sems):
    width = one.shape[1] // CHUNKS
    rows = pl.ds(halves()[part], 16)
    outs = []
    for j in range(CHUNKS):

        def body(k, _, j=j):
            at = pl.ds(pl.multiple_of(j * width + k * STEP, STEP), STEP)
            averaged = (one[:, at].astype(F32) + two[:, at].astype(F32)) * 0.25
            weight[:, at] = base[part, :, at] - (OUTER_RATE * (1.0 + NESTEROV)) * averaged
            moment[:, at] = momenta[part, :, at] + averaged
            return 0

        lax.fori_loop(0, width // STEP, body, 0, unroll=True)
        at = pl.ds(j * width, width)
        outs += [
            pltpu.make_async_copy(weight.at[:, at], weights_out.at[0, plan[1], rows, at], sems.at[j, 0]),
            pltpu.make_async_copy(moment.at[:, at], momentum_out.at[plan[1], rows, at], sems.at[j, 1]),
        ]
        for copy in outs[-2:]:
            copy.start()
    for copy in outs:
        copy.wait()


def owner_groups():
    owners = list(range(64))
    random.Random(1).shuffle(owners)

    def order(planes):
        def place(owner):
            x, y, z = owner // 16, owner // 4 % 4, owner % 4
            return planes.index(z), -min(x, 4 - x) - min(y, 4 - y)

        return sorted(owners, key=place)

    orders = (order((2, 0, 3, 1)), order((3, 0, 2, 1)))
    return [[island * 64 + owner for owner in orders[island % 2]] for island in range(4)]


def swap(x, bit):
    return lax.ppermute(x, "island", [(i, i ^ bit) for i in range(lax.axis_size("island"))])


def in_hbm(x):
    return pltpu.with_memory_space_constraint(x, pltpu.HBM)


def on_device(
    local_weights, first_moment, second_moment, gradient, anchor, outer_momentum, plan, step_count
):
    local_weights, first_moment, second_moment, gradient, anchor, outer_momentum = (
        in_hbm(x) for x in (local_weights, first_moment, second_moment, gradient, anchor, outer_momentum)
    )
    rows, columns = anchor.shape[1:]
    owners = lax.axis_size("fsdp")
    shape = jax.ShapeDtypeStruct
    dma = pltpu.SemaphoreType.DMA
    buffer = pltpu.VMEM
    two = (2, 16, columns)

    squares, chosen = call(
        squares_kernel,
        [shape((owners, 128), F32), pltpu.SMEM((2,), jnp.int32)],
        [HBM] * 2,
        [VMEM, SMEM],
        [buffer((2, rows, columns), BF16), dma((2 * PIECES,)), dma((1,))],
        (4 * rows * columns, 4 * rows * columns),
    )(in_hbm(plan), gradient)
    step_count, squares = lax.optimization_barrier((step_count, squares))
    sums = lax.all_to_all(
        squares.reshape(owners, 1, 128), ("island", "fsdp"), 0, 0, axis_index_groups=owner_groups()
    ).reshape(owners, 128)
    base, firsts, seconds, gradients = call(
        prepare_kernel,
        [shape(two, F32)] + [shape(two, BF16)] * 3,
        [SMEM] + [HBM] * 5,
        [VMEM] * 4,
        [buffer(two, F32), buffer(two, F32), dma((2, 5))],
        (HIDDEN, HIDDEN),
    )(chosen, local_weights, first_moment, second_moment, gradient, anchor)
    factors = call(factors_kernel, shape((8, 128), F32), [SMEM], VMEM, [], (HIDDEN, HIDDEN))(step_count)
    send, keep = (
        call(
            functools.partial(pseudo_kernel, part),
            shape((16, columns), BF16),
            [VMEM] * 6,
            VMEM,
            [],
            (HIDDEN, HIDDEN) if part else (12 * rows * columns, 5 * rows * columns),
        )(factors, sums, base, firsts, seconds, gradients)
        for part in (0, 1)
    )
    summed = call(
        add_kernel,
        shape((16, columns), BF16),
        [VMEM, VMEM],
        VMEM,
        [],
        (16 * columns, 96 * columns),
    )(keep, swap(send, 1))
    far, theirs = swap(summed, 2), swap(summed, 1)

    *outs, outer_base, outer_momenta = call(
        rest_kernel,
        [shape(local_weights.shape, F32), shape(anchor.shape, F32), shape(two, F32), shape(two, F32)],
        [SMEM] + [VMEM] * 3 + [HBM] * 6,
        [HBM, HBM, VMEM, VMEM],
        [
            buffer(two, F32),
            buffer(two, BF16),
            buffer(two, BF16),
            buffer(two, BF16),
            buffer(two, F32),
            buffer(two, F32),
            buffer((rows, columns), F32),
            dma((2, 6)),
            dma((4,)),
        ],
        (HIDDEN, HIDDEN),
    )(chosen, factors, sums, summed, gradient, local_weights, first_moment, second_moment, anchor, outer_momentum)

    far, outer_base = lax.optimization_barrier((far, outer_base))
    for part, one, other in ((1, summed, far), (0, theirs, swap(far, 1))):
        outs = call(
            functools.partial(outer_kernel, part),
            [shape(local_weights.shape, F32), shape(anchor.shape, F32)],
            [SMEM] + [VMEM] * 4 + [HBM] * 2,
            [HBM, HBM],
            [buffer((16, columns), F32), buffer((16, columns), F32), dma((CHUNKS, 2))],
            (HIDDEN, HIDDEN) if part else (1, 1),
            {5: 0, 6: 1},
        )(chosen, one, other, outer_base, outer_momenta, *outs)
    return tuple(outs)


def solution(mesh):
    return jax.shard_map(
        on_device,
        mesh=mesh,
        in_specs=(
            P("island", None, "fsdp", None),
            P("island", None, "fsdp", None),
            P("island", None, "fsdp", None),
            P("island", None, "fsdp", None),
            P(None, "fsdp", None),
            P(None, "fsdp", None),
            P(),
            P(),
        ),
        out_specs=(P("island", None, "fsdp", None), P(None, "fsdp", None)),
        check_vma=False,
    )
```

```python
import functools
import math
import random

import jax
import jax.numpy as jnp
from jax import lax
from jax.experimental import pallas as pl
from jax.experimental.pallas import tpu as pltpu
from jax.sharding import PartitionSpec as P

CLIP_NORM = 1.0
NORM_EPSILON = 1e-06
BETA_ONE = 0.9
BETA_TWO = 0.95
INNER_RATE = 0.03
WEIGHT_DECAY = 0.1
ADAM_EPSILON = 1e-08
OUTER_RATE = 0.7
NESTEROV = 0.9

PIECES = 4
BEFORE = 512
CHUNKS = 2
STEP = 512
VMEM_LIMIT = 16 * 1024 * 1024
HIDDEN = 40_000_000

HBM = pl.BlockSpec(memory_space=pltpu.HBM)
VMEM = pl.BlockSpec(memory_space=pltpu.VMEM)
SMEM = pl.BlockSpec(memory_space=pltpu.SMEM)
F32, BF16 = jnp.float32, jnp.bfloat16


def call(kernel, out_shape, in_specs, out_specs, scratch, cost, aliases=None):
    flops, size = cost
    return pl.pallas_call(
        kernel,
        out_shape=out_shape,
        in_specs=in_specs,
        out_specs=out_specs,
        scratch_shapes=scratch,
        input_output_aliases=aliases or {},
        compiler_params=pltpu.CompilerParams(vmem_limit_bytes=VMEM_LIMIT),
        cost_estimate=pl.CostEstimate(flops=flops, bytes_accessed=size, transcendentals=0),
    )


def spread(vector, width):
    return jnp.concatenate([jnp.broadcast_to(vector, (16, 128))] * (width // 128), axis=1)


def columns_of(k):
    return pl.ds(pl.multiple_of(k * STEP, STEP), STEP)


def factors_kernel(step, factors):
    step = jnp.full((1, 128), step[0].astype(F32))
    first = INNER_RATE / (1.0 - jnp.exp(step * math.log(BETA_ONE)))
    second = 1.0 / (1.0 - jnp.exp(step * math.log(BETA_TWO)))
    rows = (
        BETA_ONE * first,
        (1.0 - BETA_ONE) * first,
        BETA_TWO * second,
        (1.0 - BETA_TWO) * second,
    )
    factors[...] = jnp.concatenate(rows * 2, axis=0)


def adam_factors(sums_ref, factors_ref):
    square = jnp.sum(jnp.sum(sums_ref[...], axis=0, keepdims=True), axis=1, keepdims=True)
    clip = jnp.minimum(1.0, CLIP_NORM / jnp.sqrt(jnp.broadcast_to(square, (1, 128)) + NORM_EPSILON))
    return tuple(spread(row, STEP) for row in (clip, *(factors_ref[i : i + 1] for i in range(4))))


def adam_change(first, second, gradient, factors):
    clip, a, b, c, d = factors
    scaled = gradient.astype(F32) * clip
    numerator = a * first.astype(F32) + b * scaled
    square = c * second.astype(F32) + d * (scaled * scaled)
    return numerator / (square * lax.rsqrt(square) + ADAM_EPSILON)


def halves():
    core = lax.rem(lax.axis_index("island"), 2)
    return pl.multiple_of((1 - core) * 16, 16), pl.multiple_of(core * 16, 16)


def squares_kernel(plan, gradient, squares, chosen, whole, sems, plan_sem):
    plan_copy = pltpu.make_async_copy(plan, chosen, plan_sem.at[0])
    plan_copy.start()
    width = whole.shape[2] // PIECES
    pieces = [(i, pl.ds(j * width, width)) for i in range(2) for j in range(PIECES)]
    copies = []
    for n, (i, at) in enumerate(pieces):
        copies.append(pltpu.make_async_copy(gradient.at[0, i, :, at], whole.at[i, :, at], sems.at[n]))
        copies[-1].start()
    total = jnp.zeros((32, 256), F32)
    for copy, (i, at) in zip(copies, pieces, strict=True):
        copy.wait()
        for k in range(width // 256):
            block = whole[i, :, pl.ds(at.start + k * 256, 256)].astype(F32)
            total = total + block * block
    row = jnp.sum(total[:, :128] + total[:, 128:], axis=0, keepdims=True)
    squares[...] = jnp.broadcast_to(row, squares.shape)
    plan_copy.wait()


def prepare_kernel(
    plan, weights, first, second, gradient, anchor, base, firsts, seconds, gradients, weight, anchors, sems
):
    fragment = plan[1]
    copies = []
    for part, row in enumerate(halves()):
        rows = pl.ds(row, 16)
        pairs = (
            (weights.at[0, fragment, rows], weight.at[part]),
            (anchor.at[fragment, rows], anchors.at[part]),
            (first.at[0, fragment, rows], firsts.at[part]),
            (second.at[0, fragment, rows], seconds.at[part]),
            (gradient.at[0, fragment, rows], gradients.at[part]),
        )
        for i, (source, target) in enumerate(pairs):
            copies.append(pltpu.make_async_copy(source, target, sems.at[part, i]))
            copies[-1].start()
    for part in range(2):
        for copy in copies[part * 5 : part * 5 + 5]:
            copy.wait()

        def body(k, _, part=part):
            at = columns_of(k)
            decayed = (1.0 - INNER_RATE * WEIGHT_DECAY) * weight[part, :, at]
            base[part, :, at] = anchors[part, :, at] - decayed
            return 0

        lax.fori_loop(0, base.shape[2] // STEP, body, 0, unroll=True)


def pseudo_kernel(part, factors, sums, base, first, second, gradient, out):
    factors = adam_factors(sums, factors)

    def body(k, _):
        at = columns_of(k)
        change = adam_change(first[part, :, at], second[part, :, at], gradient[part, :, at], factors)
        out[:, at] = (base[part, :, at] + change).astype(BF16)
        return 0

    lax.fori_loop(0, out.shape[1] // STEP, body, 0, unroll=True)


def add_kernel(one, two, _, out):
    out[...] = (one[...].astype(F32) + two[...].astype(F32)).astype(BF16)


def late_swap():
    return lax.rem(lax.axis_index("fsdp"), 4) == 3


def rest_of(part, columns, fragment, factors, sums, gradient, weights, first, second, weights_out, scratch):
    *buffers, result, sems = scratch
    rows, cut = pl.ds(part * 16, 16), pl.ds(*columns)
    here = pl.ds(0, columns[1])
    copies = [
        pltpu.make_async_copy(source.at[0, fragment, rows, cut], buffer.at[:, here], sems.at[i])
        for i, (source, buffer) in enumerate(zip((weights, first, second, gradient), buffers, strict=True))
    ]
    for copy in copies:
        copy.start()
    factors = adam_factors(sums, factors)
    for copy in copies:
        copy.wait()

    def body(k, _):
        at = columns_of(k)
        w, m, v, g = (buffer[:, at] for buffer in buffers)
        result[:, at] = (1.0 - INNER_RATE * WEIGHT_DECAY) * w - adam_change(m, v, g, factors)
        return 0

    lax.fori_loop(0, columns[1] // STEP, body, 0, unroll=True)
    out = pltpu.make_async_copy(result.at[:, here], weights_out.at[0, fragment, rows, cut], sems.at[4])
    out.start()
    out.wait()


def rest_before_kernel(plan, *refs):
    @pl.when(late_swap())
    def _():
        rest_of(0, (0, BEFORE), 1 - plan[1], *refs[:6], refs[6], refs[7:])


def rest_beside_kernel(plan, _, anchor, momentum, *refs):
    fragment = plan[1]
    args, (weights_out, momentum_out, base, momenta) = refs[:6], refs[7:11]
    anchors, still, outer_sems, *scratch = refs[11:]
    copies = [pltpu.make_async_copy(momentum.at[1 - fragment], still, outer_sems.at[2, 0])]
    for part, row in enumerate(halves()):
        rows = pl.ds(row, 16)
        copies.append(pltpu.make_async_copy(anchor.at[fragment, rows], anchors.at[part], outer_sems.at[part, 0]))
        copies.append(pltpu.make_async_copy(momentum.at[fragment, rows], momenta.at[part], outer_sems.at[part, 1]))
    for copy in copies:
        copy.start()

    @pl.when(jnp.logical_not(late_swap()))
    def _():
        rest_of(0, (0, BEFORE), 1 - fragment, *args, weights_out, scratch)

    copies[0].wait()
    kept = pltpu.make_async_copy(still, momentum_out.at[1 - fragment], outer_sems.at[2, 1])
    kept.start()
    whole = momentum.shape[2]
    rest_of(0, (BEFORE, whole - BEFORE), 1 - fragment, *args, weights_out, scratch)
    rest_of(1, (0, whole), 1 - fragment, *args, weights_out, scratch)
    for copy in copies[1:]:
        copy.wait()
    for part in range(2):

        def outer(k, _, part=part):
            at = columns_of(k)
            m = momenta[part, :, at]
            base[part, :, at] = anchors[part, :, at] - (OUTER_RATE * NESTEROV * NESTEROV) * m
            momenta[part, :, at] = NESTEROV * m
            return 0

        lax.fori_loop(0, base.shape[2] // STEP, outer, 0, unroll=True)
    kept.wait()


def outer_kernel(part, plan, one, two, base, momenta, _, __, weights_out, momentum_out, weight, moment, sems):
    width = one.shape[1] // CHUNKS
    rows = pl.ds(halves()[part], 16)
    outs = []
    for j in range(CHUNKS):

        def body(k, _, j=j):
            at = pl.ds(pl.multiple_of(j * width + k * STEP, STEP), STEP)
            averaged = (one[:, at].astype(F32) + two[:, at].astype(F32)) * 0.25
            weight[:, at] = base[part, :, at] - (OUTER_RATE * (1.0 + NESTEROV)) * averaged
            moment[:, at] = momenta[part, :, at] + averaged
            return 0

        lax.fori_loop(0, width // STEP, body, 0, unroll=True)
        at = pl.ds(j * width, width)
        outs += [
            pltpu.make_async_copy(weight.at[:, at], weights_out.at[0, plan[1], rows, at], sems.at[j, 0]),
            pltpu.make_async_copy(moment.at[:, at], momentum_out.at[plan[1], rows, at], sems.at[j, 1]),
        ]
        for copy in outs[-2:]:
            copy.start()
    for copy in outs:
        copy.wait()


def owner_groups():
    owners = list(range(64))
    random.Random(1).shuffle(owners)

    def order(planes):
        def place(owner):
            x, y, z = owner // 16, owner // 4 % 4, owner % 4
            return planes.index(z), -min(x, 4 - x) - min(y, 4 - y)

        return sorted(owners, key=place)

    orders = (order((2, 0, 3, 1)), order((3, 0, 2, 1)))
    return [[island * 64 + owner for owner in orders[island % 2]] for island in range(4)]


def swap(x, bit):
    return lax.ppermute(x, "island", [(i, i ^ bit) for i in range(lax.axis_size("island"))])


def in_hbm(x):
    return pltpu.with_memory_space_constraint(x, pltpu.HBM)


def on_device(
    local_weights, first_moment, second_moment, gradient, anchor, outer_momentum, plan, step_count
):
    local_weights, first_moment, second_moment, gradient, anchor, outer_momentum = (
        in_hbm(x) for x in (local_weights, first_moment, second_moment, gradient, anchor, outer_momentum)
    )
    rows, columns = anchor.shape[1:]
    owners = lax.axis_size("fsdp")
    shape = jax.ShapeDtypeStruct
    dma = pltpu.SemaphoreType.DMA
    buffer = pltpu.VMEM
    two = (2, 16, columns)

    squares, chosen = call(
        squares_kernel,
        [shape((owners, 128), F32), pltpu.SMEM((2,), jnp.int32)],
        [HBM] * 2,
        [VMEM, SMEM],
        [buffer((2, rows, columns), BF16), dma((2 * PIECES,)), dma((1,))],
        (4 * rows * columns, 4 * rows * columns),
    )(in_hbm(plan), gradient)
    step_count, squares = lax.optimization_barrier((step_count, squares))
    sums = lax.all_to_all(
        squares.reshape(owners, 1, 128), ("island", "fsdp"), 0, 0, axis_index_groups=owner_groups()
    ).reshape(owners, 128)
    base, firsts, seconds, gradients = call(
        prepare_kernel,
        [shape(two, F32)] + [shape(two, BF16)] * 3,
        [SMEM] + [HBM] * 5,
        [VMEM] * 4,
        [buffer(two, F32), buffer(two, F32), dma((2, 5))],
        (HIDDEN, HIDDEN),
    )(chosen, local_weights, first_moment, second_moment, gradient, anchor)
    factors = call(factors_kernel, shape((8, 128), F32), [SMEM], VMEM, [], (HIDDEN, HIDDEN))(step_count)
    send, keep = (
        call(
            functools.partial(pseudo_kernel, part),
            shape((16, columns), BF16),
            [VMEM] * 6,
            VMEM,
            [],
            (HIDDEN, HIDDEN) if part else (12 * rows * columns, 5 * rows * columns),
        )(factors, sums, base, firsts, seconds, gradients)
        for part in (0, 1)
    )
    rest_args = (factors, sums, gradient, local_weights, first_moment, second_moment)
    half = (16, columns)
    rest_scratch = [
        buffer(half, F32),
        buffer(half, BF16),
        buffer(half, BF16),
        buffer(half, BF16),
        buffer(half, F32),
        dma((5,)),
    ]
    weights_out = shape(local_weights.shape, F32)
    begun = call(
        rest_before_kernel,
        weights_out,
        [SMEM, VMEM, VMEM] + [HBM] * 4,
        HBM,
        rest_scratch,
        (HIDDEN, HIDDEN),
    )(chosen, *rest_args)
    begun = in_hbm(begun)
    summed = call(
        add_kernel,
        shape(half, BF16),
        [VMEM, VMEM, HBM],
        VMEM,
        [],
        (16 * columns, 96 * columns),
    )(keep, swap(send, 1), begun)
    far, theirs = swap(summed, 2), swap(summed, 1)

    *outs, outer_base, outer_momenta = call(
        rest_beside_kernel,
        [weights_out, shape(anchor.shape, F32), shape(two, F32), shape(two, F32)],
        [SMEM, VMEM, HBM, HBM, VMEM, VMEM] + [HBM] * 5,
        [HBM, HBM, VMEM, VMEM],
        [buffer(two, F32), buffer((rows, columns), F32), dma((3, 2)), *rest_scratch],
        (HIDDEN, HIDDEN),
        {10: 0},
    )(chosen, summed, anchor, outer_momentum, *rest_args, begun)

    far, outer_base = lax.optimization_barrier((far, outer_base))
    for part, one, other in ((1, summed, far), (0, theirs, swap(far, 1))):
        outs = call(
            functools.partial(outer_kernel, part),
            [shape(local_weights.shape, F32), shape(anchor.shape, F32)],
            [SMEM] + [VMEM] * 4 + [HBM] * 2,
            [HBM, HBM],
            [buffer((16, columns), F32), buffer((16, columns), F32), dma((CHUNKS, 2))],
            (HIDDEN, HIDDEN) if part else (1, 1),
            {5: 0, 6: 1},
        )(chosen, one, other, outer_base, outer_momenta, *outs)
    return tuple(outs)


def solution(mesh):
    return jax.shard_map(
        on_device,
        mesh=mesh,
        in_specs=(
            P("island", None, "fsdp", None),
            P("island", None, "fsdp", None),
            P("island", None, "fsdp", None),
            P("island", None, "fsdp", None),
            P(None, "fsdp", None),
            P(None, "fsdp", None),
            P(),
            P(),
        ),
        out_specs=(P("island", None, "fsdp", None), P(None, "fsdp", None)),
        check_vma=False,
    )
```

```python
import functools
import math
import random

import jax
import jax.numpy as jnp
from jax import lax
from jax.experimental import pallas as pl
from jax.experimental.pallas import tpu as pltpu
from jax.sharding import PartitionSpec as P

CLIP_NORM = 1.0
NORM_EPSILON = 1e-06
BETA_ONE = 0.9
BETA_TWO = 0.95
INNER_RATE = 0.03
WEIGHT_DECAY = 0.1
ADAM_EPSILON = 1e-08
OUTER_RATE = 0.7
NESTEROV = 0.9

PIECES = 4
BEFORE = 512
CHUNKS = 2
STEP = 512
VMEM_LIMIT = 16 * 1024 * 1024
HIDDEN = 40_000_000

HBM = pl.BlockSpec(memory_space=pltpu.HBM)
VMEM = pl.BlockSpec(memory_space=pltpu.VMEM)
SMEM = pl.BlockSpec(memory_space=pltpu.SMEM)
F32, BF16 = jnp.float32, jnp.bfloat16


def call(kernel, out_shape, in_specs, out_specs, scratch, cost, aliases=None):
    flops, size = cost
    return pl.pallas_call(
        kernel,
        out_shape=out_shape,
        in_specs=in_specs,
        out_specs=out_specs,
        scratch_shapes=scratch,
        input_output_aliases=aliases or {},
        compiler_params=pltpu.CompilerParams(vmem_limit_bytes=VMEM_LIMIT),
        cost_estimate=pl.CostEstimate(flops=flops, bytes_accessed=size, transcendentals=0),
    )


def spread(vector, width):
    return jnp.concatenate([jnp.broadcast_to(vector, (16, 128))] * (width // 128), axis=1)


def columns_of(k):
    return pl.ds(pl.multiple_of(k * STEP, STEP), STEP)


def factors_kernel(step, factors):
    step = jnp.full((1, 128), step[0].astype(F32))
    first = INNER_RATE / (1.0 - jnp.exp(step * math.log(BETA_ONE)))
    second = 1.0 / (1.0 - jnp.exp(step * math.log(BETA_TWO)))
    rows = (
        BETA_ONE * first,
        (1.0 - BETA_ONE) * first,
        BETA_TWO * second,
        (1.0 - BETA_TWO) * second,
    )
    factors[...] = jnp.concatenate(rows * 2, axis=0)


def adam_factors(sums_ref, factors_ref):
    square = jnp.sum(jnp.sum(sums_ref[...], axis=0, keepdims=True), axis=1, keepdims=True)
    clip = jnp.minimum(1.0, CLIP_NORM / jnp.sqrt(jnp.broadcast_to(square, (1, 128)) + NORM_EPSILON))
    return tuple(spread(row, STEP) for row in (clip, *(factors_ref[i : i + 1] for i in range(4))))


def adam_change(first, second, gradient, factors):
    clip, a, b, c, d = factors
    scaled = gradient.astype(F32) * clip
    numerator = a * first.astype(F32) + b * scaled
    square = c * second.astype(F32) + d * (scaled * scaled)
    return numerator / (square * lax.rsqrt(square) + ADAM_EPSILON)


def halves():
    core = lax.rem(lax.axis_index("island"), 2)
    return pl.multiple_of((1 - core) * 16, 16), pl.multiple_of(core * 16, 16)


def squares_kernel(plan, gradient, squares, chosen, whole, sems, plan_sem):
    plan_copy = pltpu.make_async_copy(plan, chosen, plan_sem.at[0])
    plan_copy.start()
    width = whole.shape[2] // PIECES
    pieces = [(i, pl.ds(j * width, width)) for i in range(2) for j in range(PIECES)]
    copies = []
    for n, (i, at) in enumerate(pieces):
        copies.append(pltpu.make_async_copy(gradient.at[0, i, :, at], whole.at[i, :, at], sems.at[n]))
        copies[-1].start()
    total = jnp.zeros((32, 256), F32)
    for copy, (i, at) in zip(copies, pieces, strict=True):
        copy.wait()
        for k in range(width // 256):
            block = whole[i, :, pl.ds(at.start + k * 256, 256)].astype(F32)
            total = total + block * block
    row = jnp.sum(total[:, :128] + total[:, 128:], axis=0, keepdims=True)
    squares[...] = jnp.broadcast_to(row, squares.shape)
    plan_copy.wait()


def prepare_kernel(
    plan, weights, first, second, gradient, anchor, base, firsts, seconds, gradients, weight, anchors, sems
):
    fragment = plan[1]
    copies = []
    for part, row in enumerate(halves()):
        rows = pl.ds(row, 16)
        pairs = (
            (weights.at[0, fragment, rows], weight.at[part]),
            (anchor.at[fragment, rows], anchors.at[part]),
            (first.at[0, fragment, rows], firsts.at[part]),
            (second.at[0, fragment, rows], seconds.at[part]),
            (gradient.at[0, fragment, rows], gradients.at[part]),
        )
        for i, (source, target) in enumerate(pairs):
            copies.append(pltpu.make_async_copy(source, target, sems.at[part, i]))
            copies[-1].start()
    for part in range(2):
        for copy in copies[part * 5 : part * 5 + 5]:
            copy.wait()

        def body(k, _, part=part):
            at = columns_of(k)
            decayed = (1.0 - INNER_RATE * WEIGHT_DECAY) * weight[part, :, at]
            base[part, :, at] = anchors[part, :, at] - decayed
            return 0

        lax.fori_loop(0, base.shape[2] // STEP, body, 0, unroll=True)


def pseudo_kernel(part, factors, sums, base, first, second, gradient, out):
    factors = adam_factors(sums, factors)

    def body(k, _):
        at = columns_of(k)
        change = adam_change(first[part, :, at], second[part, :, at], gradient[part, :, at], factors)
        out[:, at] = (base[part, :, at] + change).astype(BF16)
        return 0

    lax.fori_loop(0, out.shape[1] // STEP, body, 0, unroll=True)


def add_kernel(one, two, _, out):
    out[...] = (one[...].astype(F32) + two[...].astype(F32)).astype(BF16)


def late_swap():
    return jnp.logical_and(lax.rem(lax.axis_index("fsdp"), 4) == 3, lax.axis_index("island") < 2)


def rest_of(part, columns, fragment, factors, sums, gradient, weights, first, second, weights_out, scratch):
    *buffers, result, sems = scratch
    rows, cut = pl.ds(part * 16, 16), pl.ds(*columns)
    here = pl.ds(0, columns[1])
    copies = [
        pltpu.make_async_copy(source.at[0, fragment, rows, cut], buffer.at[:, here], sems.at[i])
        for i, (source, buffer) in enumerate(zip((weights, first, second, gradient), buffers, strict=True))
    ]
    for copy in copies:
        copy.start()
    factors = adam_factors(sums, factors)
    for copy in copies:
        copy.wait()

    def body(k, _):
        at = columns_of(k)
        w, m, v, g = (buffer[:, at] for buffer in buffers)
        result[:, at] = (1.0 - INNER_RATE * WEIGHT_DECAY) * w - adam_change(m, v, g, factors)
        return 0

    lax.fori_loop(0, columns[1] // STEP, body, 0, unroll=True)
    out = pltpu.make_async_copy(result.at[:, here], weights_out.at[0, fragment, rows, cut], sems.at[4])
    out.start()
    out.wait()


def rest_before_kernel(plan, *refs):
    @pl.when(late_swap())
    def _():
        rest_of(0, (0, BEFORE), 1 - plan[1], *refs[:6], refs[6], refs[7:])


def rest_beside_kernel(plan, _, anchor, momentum, *refs):
    fragment = plan[1]
    args, (weights_out, momentum_out, base, momenta) = refs[:6], refs[7:11]
    anchors, still, outer_sems, *scratch = refs[11:]
    copies = [pltpu.make_async_copy(momentum.at[1 - fragment], still, outer_sems.at[2, 0])]
    for part, row in enumerate(halves()):
        rows = pl.ds(row, 16)
        copies.append(pltpu.make_async_copy(anchor.at[fragment, rows], anchors.at[part], outer_sems.at[part, 0]))
        copies.append(pltpu.make_async_copy(momentum.at[fragment, rows], momenta.at[part], outer_sems.at[part, 1]))
    for copy in copies:
        copy.start()

    @pl.when(jnp.logical_not(late_swap()))
    def _():
        rest_of(0, (0, BEFORE), 1 - fragment, *args, weights_out, scratch)

    copies[0].wait()
    kept = pltpu.make_async_copy(still, momentum_out.at[1 - fragment], outer_sems.at[2, 1])
    kept.start()
    whole = momentum.shape[2]
    rest_of(0, (BEFORE, whole - BEFORE), 1 - fragment, *args, weights_out, scratch)
    rest_of(1, (0, whole), 1 - fragment, *args, weights_out, scratch)
    for copy in copies[1:]:
        copy.wait()
    for part in range(2):

        def outer(k, _, part=part):
            at = columns_of(k)
            m = momenta[part, :, at]
            base[part, :, at] = anchors[part, :, at] - (OUTER_RATE * NESTEROV * NESTEROV) * m
            momenta[part, :, at] = NESTEROV * m
            return 0

        lax.fori_loop(0, base.shape[2] // STEP, outer, 0, unroll=True)
    kept.wait()


def outer_kernel(part, plan, one, two, base, momenta, _, __, weights_out, momentum_out, weight, moment, sems):
    width = one.shape[1] // CHUNKS
    rows = pl.ds(halves()[part], 16)
    outs = []
    for j in range(CHUNKS):

        def body(k, _, j=j):
            at = pl.ds(pl.multiple_of(j * width + k * STEP, STEP), STEP)
            averaged = (one[:, at].astype(F32) + two[:, at].astype(F32)) * 0.25
            weight[:, at] = base[part, :, at] - (OUTER_RATE * (1.0 + NESTEROV)) * averaged
            moment[:, at] = momenta[part, :, at] + averaged
            return 0

        lax.fori_loop(0, width // STEP, body, 0, unroll=True)
        at = pl.ds(j * width, width)
        outs += [
            pltpu.make_async_copy(weight.at[:, at], weights_out.at[0, plan[1], rows, at], sems.at[j, 0]),
            pltpu.make_async_copy(moment.at[:, at], momentum_out.at[plan[1], rows, at], sems.at[j, 1]),
        ]
        for copy in outs[-2:]:
            copy.start()
    for copy in outs:
        copy.wait()


def owner_groups():
    owners = list(range(64))
    random.Random(1).shuffle(owners)

    def order(planes):
        def place(owner):
            x, y, z = owner // 16, owner // 4 % 4, owner % 4
            return planes.index(z), -min(x, 4 - x) - min(y, 4 - y)

        return sorted(owners, key=place)

    orders = (order((2, 0, 3, 1)), order((3, 0, 2, 1)))
    return [[island * 64 + owner for owner in orders[island % 2]] for island in range(4)]


def swap(x, bit):
    return lax.ppermute(x, "island", [(i, i ^ bit) for i in range(lax.axis_size("island"))])


def in_hbm(x):
    return pltpu.with_memory_space_constraint(x, pltpu.HBM)


def on_device(
    local_weights, first_moment, second_moment, gradient, anchor, outer_momentum, plan, step_count
):
    local_weights, first_moment, second_moment, gradient, anchor, outer_momentum = (
        in_hbm(x) for x in (local_weights, first_moment, second_moment, gradient, anchor, outer_momentum)
    )
    rows, columns = anchor.shape[1:]
    owners = lax.axis_size("fsdp")
    shape = jax.ShapeDtypeStruct
    dma = pltpu.SemaphoreType.DMA
    buffer = pltpu.VMEM
    two = (2, 16, columns)

    squares, chosen = call(
        squares_kernel,
        [shape((owners, 128), F32), pltpu.SMEM((2,), jnp.int32)],
        [HBM] * 2,
        [VMEM, SMEM],
        [buffer((2, rows, columns), BF16), dma((2 * PIECES,)), dma((1,))],
        (4 * rows * columns, 4 * rows * columns),
    )(in_hbm(plan), gradient)
    step_count, squares = lax.optimization_barrier((step_count, squares))
    sums = lax.all_to_all(
        squares.reshape(owners, 1, 128), ("island", "fsdp"), 0, 0, axis_index_groups=owner_groups()
    ).reshape(owners, 128)
    base, firsts, seconds, gradients = call(
        prepare_kernel,
        [shape(two, F32)] + [shape(two, BF16)] * 3,
        [SMEM] + [HBM] * 5,
        [VMEM] * 4,
        [buffer(two, F32), buffer(two, F32), dma((2, 5))],
        (HIDDEN, HIDDEN),
    )(chosen, local_weights, first_moment, second_moment, gradient, anchor)
    factors = call(factors_kernel, shape((8, 128), F32), [SMEM], VMEM, [], (HIDDEN, HIDDEN))(step_count)
    send, keep = (
        call(
            functools.partial(pseudo_kernel, part),
            shape((16, columns), BF16),
            [VMEM] * 6,
            VMEM,
            [],
            (HIDDEN, HIDDEN) if part else (12 * rows * columns, 5 * rows * columns),
        )(factors, sums, base, firsts, seconds, gradients)
        for part in (0, 1)
    )
    rest_args = (factors, sums, gradient, local_weights, first_moment, second_moment)
    half = (16, columns)
    rest_scratch = [
        buffer(half, F32),
        buffer(half, BF16),
        buffer(half, BF16),
        buffer(half, BF16),
        buffer(half, F32),
        dma((5,)),
    ]
    weights_out = shape(local_weights.shape, F32)
    begun = call(
        rest_before_kernel,
        weights_out,
        [SMEM, VMEM, VMEM] + [HBM] * 4,
        HBM,
        rest_scratch,
        (HIDDEN, HIDDEN),
    )(chosen, *rest_args)
    begun = in_hbm(begun)
    summed = call(
        add_kernel,
        shape(half, BF16),
        [VMEM, VMEM, HBM],
        VMEM,
        [],
        (16 * columns, 96 * columns),
    )(keep, swap(send, 1), begun)
    far, theirs = swap(summed, 2), swap(summed, 1)

    *outs, outer_base, outer_momenta = call(
        rest_beside_kernel,
        [weights_out, shape(anchor.shape, F32), shape(two, F32), shape(two, F32)],
        [SMEM, VMEM, HBM, HBM, VMEM, VMEM] + [HBM] * 5,
        [HBM, HBM, VMEM, VMEM],
        [buffer(two, F32), buffer((rows, columns), F32), dma((3, 2)), *rest_scratch],
        (HIDDEN, HIDDEN),
        {10: 0},
    )(chosen, summed, anchor, outer_momentum, *rest_args, begun)

    far, outer_base = lax.optimization_barrier((far, outer_base))
    for part, one, other in ((1, summed, far), (0, theirs, swap(far, 1))):
        outs = call(
            functools.partial(outer_kernel, part),
            [shape(local_weights.shape, F32), shape(anchor.shape, F32)],
            [SMEM] + [VMEM] * 4 + [HBM] * 2,
            [HBM, HBM],
            [buffer((16, columns), F32), buffer((16, columns), F32), dma((CHUNKS, 2))],
            (HIDDEN, HIDDEN) if part else (1, 1),
            {5: 0, 6: 1},
        )(chosen, one, other, outer_base, outer_momenta, *outs)
    return tuple(outs)


def solution(mesh):
    return jax.shard_map(
        on_device,
        mesh=mesh,
        in_specs=(
            P("island", None, "fsdp", None),
            P("island", None, "fsdp", None),
            P("island", None, "fsdp", None),
            P("island", None, "fsdp", None),
            P(None, "fsdp", None),
            P(None, "fsdp", None),
            P(),
            P(),
        ),
        out_specs=(P("island", None, "fsdp", None), P(None, "fsdp", None)),
        check_vma=False,
    )
```
